256 devices in a mesh: grp: 2 (over x_hi), dp: 8 (over y, core), mp: 16 (over x_lo, z).
Axes of the slice: x: 4 (x_hi: 2, x_lo: 2; x = x_hi * 2 + x_lo), y: 4, z: 8, core: 2. Of those that a mesh axis runs over, the one named last changes fastest.
Arguments:
- hidden_in: bfloat16 [1024, 8192], P('dp'), may hold values from -6 to 6
- full_weights: bfloat16 [8192, 2, 16384], P('mp', 'grp', 'dp'), may hold values from -1 to 1, as said below
- codes: int32 [8192, 2, 16384], P('mp', None, 'dp'), may hold values from 0 to 3, as said below
- scales: float32 [64, 2, 16384], P('mp', None, 'dp'), may hold values from 0 to 1, as said below
Outputs:
- scale_grad: float32 [64, 2, 16384], P('mp', 'grp', 'dp')
The draws below stay inside these ranges and needn't reach their ends.
Inputs may be any that keep to these rules, and one draw needn't show every extreme that they name: codes are 2-bit values. full_weights lie near the grid that codes and positive group scales span. scales are positive.
All inputs are finite; a program needn't handle non-finite values.
Results may differ from the reference program's by a relative error of at most 0.0088.
Values may be sent and summed in bfloat16 or wider, within the bound.
A program may use at most 128 MiB of HBM per device.

```python
import jax
import jax.numpy as jnp
from jax import lax

D = 8192
FF = 16384
GROUP = 128
TOKENS = 1024
N_MP = 16


def teacher_grid(key):
    grid_codes = jax.random.randint(jax.random.fold_in(key, 71), (D, 2, FF), 0, 4).astype(jnp.int32)
    log_scale = jax.random.uniform(jax.random.fold_in(key, 72), (D // GROUP, 2, FF), jnp.float32, -0.7, 0.7)
    base = jnp.exp(log_scale) / jnp.sqrt(jnp.float32(D))
    return (grid_codes, base)


def draw_codes(key, part):
    grid_codes, base = teacher_grid(key)
    return grid_codes


def draw_full_weights(key, part):
    grid_codes, base = teacher_grid(key)
    key = jax.random.fold_in(key, 2)
    noise = 0.35 * jax.random.truncated_normal(key, -3.0, 3.0, (D, 2, FF), jnp.float32)
    values = jnp.repeat(base, GROUP, axis=0) * (grid_codes.astype(jnp.float32) - 1.5 + noise)
    return values.astype(jnp.bfloat16)


def draw_scales(key, part):
    grid_codes, base = teacher_grid(key)
    key = jax.random.fold_in(key, 3)
    factor = jnp.exp(jax.random.uniform(key, (D // GROUP, 2, FF), jnp.float32, -0.5, 0.47))
    return base * factor


def shard_levels(rng, dims, pieces, smallest, high):
    def one(axis_at, blocks):
        steps = jax.random.uniform(jax.random.fold_in(jax.random.fold_in(rng, 6), axis_at), (blocks,), jnp.float32, smallest / len(pieces), high / len(pieces))
        return jnp.repeat(jnp.exp(steps), dims[axis_at] // blocks).reshape((-1,) + (1,) * (len(dims) - axis_at - 1))

    gain = one(*pieces[0])
    for cut in pieces[1:]:
        gain = gain * one(*cut)
    return gain


def centred(stream_key, extent, width, limit, cuts=(), kind=jnp.bfloat16):
    values = jax.random.normal(stream_key, extent, jnp.float32) * width
    if len(cuts) > 0:
        values = shard_levels(stream_key, extent, cuts, -0.22, 0.18) * values
    return jnp.clip(values, min=-limit, max=limit).astype(kind)


def setup_inputs(seed: int = 0) -> dict:
    key_list = jax.random.split(jax.random.key(seed), 5)
    return {
        "hidden_in": centred(key_list[0], (TOKENS, D), 1.0, 6.0, ((0, 8),)),
        "full_weights": draw_full_weights(jax.random.fold_in(key_list[4], 71), 0),
        "codes": draw_codes(jax.random.fold_in(key_list[4], 71), 0),
        "scales": draw_scales(jax.random.fold_in(key_list[4], 71), 0),
    }


def project(hidden_in, weights):
    block = D // N_MP
    flat = weights.reshape(D, 2 * FF)

    def add_block(index, total):
        start = (index * block).astype(jnp.int32)
        rows = lax.dynamic_slice_in_dim(hidden_in, start, block, 1)
        cols = lax.dynamic_slice_in_dim(flat, start, block, 0)
        return total + jnp.dot(rows, cols, preferred_element_type=jnp.float32)

    total = jnp.zeros((TOKENS, 2 * FF), jnp.float32)
    total = lax.fori_loop(jnp.int32(0), jnp.int32(N_MP), add_block, total)
    return total.reshape(TOKENS, 2, FF)


def reference(hidden_in, full_weights, codes, scales):
    offsets = codes.astype(jnp.float32) - 1.5
    student_weights = (jnp.repeat(scales, GROUP, axis=0) * offsets).astype(jnp.bfloat16)
    teacher_proj = project(hidden_in, full_weights)
    student_proj = project(hidden_in, student_weights)
    teacher_hidden = jax.nn.silu(teacher_proj[:, 0]) * teacher_proj[:, 1]
    gate = student_proj[:, 0]
    upper = student_proj[:, 1]
    student_hidden = jax.nn.silu(gate) * upper
    difference = (student_hidden - teacher_hidden) / TOKENS
    sig = jax.nn.sigmoid(gate)
    grad_gate = (difference * upper * sig * (1.0 + gate * (1.0 - sig))).astype(jnp.bfloat16)
    grad_up = (difference * gate * sig).astype(jnp.bfloat16)
    results = []
    for half, grads in ((0, grad_gate), (1, grad_up)):
        weight_grads = jnp.dot(hidden_in.T, grads, preferred_element_type=jnp.float32)
        summed = (weight_grads * offsets[:, half, :]).reshape(D // GROUP, GROUP, FF).sum(axis=1)
        results.append(summed)
    return jnp.stack(results, axis=1)
```

```python
import jax
import jax.numpy as jnp
from jax import lax
from jax.experimental import pallas as pl
from jax.experimental.pallas import tpu as pltpu
from jax.sharding import PartitionSpec as P

BF = jnp.bfloat16
F32 = jnp.float32
CHUNKS = 4
PERIOD = 3


def multiple(value, of=128):
    return pl.multiple_of(value, of)


def sigmoid(v):
    return 1.0 / (1.0 + jnp.exp(-v))


def kernel(
    hidden, full, codes, scales, out,
    x_all, x_turned, w_teacher, offsets, w_student, code_own, code_next, code_prev,
    scale_all, scale_in, send_offsets, partial, stage, landed, grads, results, gathered,
    local_sem, x_send, x_recv, t_send, t_recv, s_send, s_recv, c_send, c_recv,
    r_send, r_recv, g_send, g_recv, o_send, o_recv,
):
    hi = lax.axis_index("grp")
    dp = lax.axis_index("dp")
    mp = lax.axis_index("mp")
    lo, z = mp // 8, lax.rem(mp, 8)
    y, core = dp // 2, lax.rem(dp, 2)
    x = hi * 2 + lo
    way = 1 - 2 * core

    def at(x=x, y=y, z=z, core=core):
        return (x // 2, y * 2 + core, lax.rem(x, 2) * 8 + z)

    x_next, x_prev, x_far = lax.rem(x + 1, 4), lax.rem(x + 3, 4), lax.rem(x + 2, 4)
    y_fwd, y_bwd, y_far = lax.rem(y + 4 + way, 4), lax.rem(y + 4 - way, 4), lax.rem(y + 2, 4)

    def zed(step):
        return lax.rem(z + 8 + way * step, 8)

    sibling = at(core=1 - core)
    to_y_fwd, to_y_bwd = at(y=y_fwd), at(y=y_bwd)
    to_x = [at(x=x_next), at(x=x_prev), at(x=x_far)]
    x_of = [x_next, x_prev, x_far]
    to_z_fwd, to_z_bwd = at(z=zed(1)), at(z=zed(-1))

    sent = []

    def send(src, dst, send_sem, recv_sem, device):
        copy = pltpu.make_async_remote_copy(
            src_ref=src, dst_ref=dst, send_sem=send_sem, recv_sem=recv_sem,
            device_id=device, device_id_type=pl.DeviceIdType.MESH,
        )
        copy.start()
        sent.append(copy)

    def arrived(ref, send_sem, recv_sem):
        pltpu.make_async_remote_copy(
            src_ref=ref, dst_ref=ref, send_sem=send_sem, recv_sem=recv_sem,
            device_id=sibling, device_id_type=pl.DeviceIdType.MESH,
        ).wait_recv()

    def local(src, dst, index):
        copy = pltpu.make_async_copy(src, dst, local_sem.at[index])
        copy.start()
        return copy

    def token_rows(block):
        return x_all.at[pl.ds(multiple(block * 128), 128), :]

    def own_columns(ref, chunk):
        return ref.at[chunk, lo, :, pl.ds(multiple(hi * 128), 128)]

    def teacher_columns(which, chunk):
        return full.at[:, pl.ds(multiple(which * 512 + chunk * 128), 128)]

    hidden_copies = [
        local(
            hidden.at[:, pl.ds(multiple(z * 512 + half * 4096), 512)],
            x_all.at[pl.ds(multiple(dp * 128), 128), pl.ds(half * 512, 512)],
            half,
        )
        for half in range(2)
    ]
    next_copy = local(codes.at[:, x_next], code_next, 2)
    prev_copy = local(codes.at[:, x_prev], code_prev, 3)
    scale_copy = local(scales, scale_in, 4)
    own_copy = local(codes.at[:, x], code_own, 5)
    teacher_copies = [
        local(teacher_columns(x, c), own_columns(w_teacher, c), 6 + c) for c in range(CHUNKS)
    ]

    barrier = pltpu.get_barrier_semaphore()
    for device in [sibling, to_y_fwd, to_y_bwd, to_z_fwd, to_z_bwd] + to_x:
        pl.semaphore_signal(barrier, inc=1, device_id=device, device_id_type=pl.DeviceIdType.MESH)
    pl.semaphore_wait(barrier, 8)

    def send_teacher(c):
        for j in (2, 0, 1):
            send(teacher_columns(x_of[j], c), own_columns(w_teacher, c),
                 t_send.at[c, j], t_recv.at[c, j], to_x[j])

    def code_offsets(ref, c, k):
        rows = ref.reshape(512 * 8, 128)[pl.ds(c * 2 + k, 512, stride=8), :]
        return (rows.astype(F32) - 1.5).astype(BF)

    def send_student(c):
        for j, ref in ((0, code_next), (1, code_prev)):
            low, high = code_offsets(ref, c, 0), code_offsets(ref, c, 1)
            send_offsets[c, j] = jnp.where(hi == 0, low, high)
            send(send_offsets.at[c, j], own_columns(offsets, c),
                 s_send.at[c, j], s_recv.at[c, j], to_x[j])

    def own_offsets(c):
        for k in range(2):
            offsets[c, lo, :, k * 128:(k + 1) * 128] = code_offsets(code_own, c, k)

    send_teacher(0)
    for copy in hidden_copies:
        copy.wait()
    mine = token_rows(dp)
    send(mine, mine, x_send.at[0], x_recv.at[0], to_y_fwd)
    send(mine, mine, x_send.at[1], x_recv.at[1], to_y_bwd)
    send(mine, mine, x_send.at[2], x_recv.at[2], sibling)
    next_copy.wait()
    prev_copy.wait()
    send_student(0)
    scale_copy.wait()
    scale_all[lo] = scale_in[:, x]
    send(scale_in.at[:, x_next], scale_all.at[lo], c_send, c_recv, to_x[0])
    send_teacher(1)
    send_student(1)
    own_copy.wait()
    for c in range(CHUNKS):
        own_offsets(c)

    behind, ahead, far = (token_rows(b * 2 + core) for b in (y_bwd, y_fwd, y_far))
    arrived(behind, x_send.at[0], x_recv.at[0])
    send(behind, behind, x_send.at[3], x_recv.at[3], to_y_fwd)
    send(behind, behind, x_send.at[4], x_recv.at[4], sibling)
    arrived(ahead, x_send.at[1], x_recv.at[1])
    send(ahead, ahead, x_send.at[5], x_recv.at[5], sibling)
    arrived(far, x_send.at[3], x_recv.at[3])
    send(far, far, x_send.at[6], x_recv.at[6], sibling)
    other = 1 - core
    for b, i in ((y, 2), (y_fwd, 4), (y_bwd, 5), (y_far, 6)):
        arrived(token_rows(b * 2 + other), x_send.at[i], x_recv.at[i])

    def project(c):
        teacher_copies[c].wait()
        for j, origin in ((0, x_prev), (1, x_next), (2, x_far)):
            block = w_teacher.at[
                c, lax.rem(origin, 2), :, pl.ds(multiple((origin // 2) * 128), 128)
            ]
            arrived(block, t_send.at[c, j], t_recv.at[c, j])
        for j, origin in ((0, x_prev), (1, x_next)):
            block = offsets.at[
                c, lax.rem(origin, 2), :, pl.ds(multiple((origin // 2) * 128), 128)
            ]
            arrived(block, s_send.at[c, j], s_recv.at[c, j])
        if c == 0:
            arrived(scale_all.at[1 - lo], c_send, c_recv)
        if c + 2 < CHUNKS:
            send_teacher(c + 2)
            send_student(c + 2)
        for half in range(2):
            for group in range(4):
                line = jnp.concatenate(
                    [scale_all[half, group, c * 2 + k:c * 2 + k + 1, :] for k in range(2)], axis=1
                )
                rows = pl.ds(half * 512 + group * 128, 128)
                values = offsets[c, half, group * 128:(group + 1) * 128, :].astype(F32)
                w_student[rows, :] = (values * line).astype(BF)
        teacher = w_teacher.at[c].reshape(1024, 256)

        @pl.loop(0, 4)
        def _(i):
            tokens = x_all[pl.ds(multiple(i * 256, 256), 256), :]
            student_part = jnp.dot(tokens, w_student[...], preferred_element_type=F32)
            teacher_part = jnp.dot(tokens, teacher[...], preferred_element_type=F32)
            gap = student_part - teacher_part
            for h in range(2):
                part = slice(h * 128, (h + 1) * 128)
                partial[c, i * 2 + h, :, 0:256] = student_part[part]
                partial[c, i * 2 + h, :, 256:512] = gap[part]

        pass_on(c, 0, zed(4), None, to_z_fwd)
        pass_on(c, 4, zed(-3), None, to_z_bwd)

    def pass_on(c, index, owner, before, device):
        total = partial[c, owner]
        if before is not None:
            total = total + landed[c, before].astype(F32)
        stage[c, index] = total.astype(BF)
        send(stage.at[c, index], landed.at[c, index],
             r_send.at[c, index], r_recv.at[c, index], device)

    def summed(c, index):
        arrived(landed.at[c, index], r_send.at[c, index], r_recv.at[c, index])

    def reduce_step(c, step):
        summed(c, step - 1)
        if step < 4:
            pass_on(c, step, zed(4 - step), step - 1, to_z_fwd)
            summed(c, 3 + step)
            if step < 3:
                pass_on(c, 4 + step, zed(step - 3), 3 + step, to_z_bwd)
            return
        total = partial[c, z] + landed[c, 3].astype(F32) + landed[c, 6].astype(F32)
        gate, upper = total[:, 0:128], total[:, 128:256]
        teacher_gate, teacher_upper = gate - total[:, 256:384], upper - total[:, 384:512]
        sig = sigmoid(gate)
        student_hidden = gate * sig * upper
        teacher_hidden = teacher_gate * sigmoid(teacher_gate) * teacher_upper
        difference = (student_hidden - teacher_hidden) * (1.0 / 1024.0)
        grads[c, z, :, 0:128] = (difference * upper * sig * (1.0 + gate * (1.0 - sig))).astype(BF)
        grads[c, z, :, 128:256] = (difference * gate * sig).astype(BF)
        own = grads.at[c, z]
        send(own, own, g_send.at[c, 0], g_recv.at[c, 0], to_z_fwd)
        send(own, own, g_send.at[c, 4], g_recv.at[c, 4], to_z_bwd)

    def gather_step(c, step):
        block = grads.at[c, zed(-step)]
        arrived(block, g_send.at[c, step - 1], g_recv.at[c, step - 1])
        if step < 4:
            send(block, block, g_send.at[c, step], g_recv.at[c, step], to_z_fwd)
            block = grads.at[c, zed(step)]
            arrived(block, g_send.at[c, 3 + step], g_recv.at[c, 3 + step])
            if step < 3:
                send(block, block, g_send.at[c, 4 + step], g_recv.at[c, 4 + step], to_z_bwd)

    def turn():
        for i in range(8):
            rows = slice(i * 128, (i + 1) * 128)
            x_turned[:, rows] = x_all[rows, :].T

    def back(c):
        all_grads = grads.at[c].reshape(1024, 256)
        for half in range(2):
            rows = x_turned[half * 512:(half + 1) * 512, :]
            weight_grads = jnp.dot(rows, all_grads[...], preferred_element_type=F32)
            weighted = weight_grads * offsets[c, half].astype(F32)
            sums = weighted.reshape(4, 128, 256).sum(axis=1)
            for k in range(2):
                results[k, half, :, c * 128:(c + 1) * 128] = sums[:, k * 128:(k + 1) * 128]

    events = []
    for c in range(CHUNKS):
        start = c * PERIOD
        events.append((start, c, project, ()))
        for step in range(1, 5):
            events.append((start + step, c, reduce_step, (step,)))
            events.append((start + 4 + step, c, gather_step, (step,)))
        events.append((start + 9, c, back, ()))
    turned = False
    for _, c, action, rest in sorted(events, key=lambda e: e[:2]):
        action(c, *rest)
        if not turned:
            turn()
            turned = True

    for j in range(3):
        send(results.at[x_of[j] // 2, lax.rem(x_of[j], 2)], gathered.at[x],
             o_send.at[j], o_recv.at[j], to_x[j])
    gathered[x] = results[hi, lo]
    for j, origin in ((0, x_prev), (1, x_next), (2, x_far)):
        arrived(gathered.at[origin], o_send.at[j], o_recv.at[j])
    for i in range(4):
        out[:, i * 512:(i + 1) * 512] = gathered[i]
    for copy in sent:
        copy.wait_send()


def tiles_of(array):
    rows = array.shape[0]
    return array.reshape(rows, 2, 4, 4, 128).transpose(0, 2, 3, 1, 4).reshape(rows, 4, 8, 128)


def per_device(hidden_in, full_weights, codes, scales):
    dma = pltpu.SemaphoreType.DMA
    out = pl.pallas_call(
        kernel,
        out_shape=jax.ShapeDtypeStruct((4, 2048), F32),
        in_specs=[pl.BlockSpec(memory_space=pl.ANY)] * 4,
        out_specs=pl.BlockSpec(memory_space=pltpu.VMEM),
        scratch_shapes=[
            pltpu.VMEM((1024, 1024), BF),
            pltpu.VMEM((1024, 1024), BF),
            pltpu.VMEM((CHUNKS, 2, 512, 256), BF),
            pltpu.VMEM((CHUNKS, 2, 512, 256), BF),
            pltpu.VMEM((1024, 256), BF),
            pltpu.VMEM((512, 8, 128), jnp.int32),
            pltpu.VMEM((512, 8, 128), jnp.int32),
            pltpu.VMEM((512, 8, 128), jnp.int32),
            pltpu.VMEM((2, 4, 8, 128), F32),
            pltpu.VMEM((4, 4, 8, 128), F32),
            pltpu.VMEM((CHUNKS, 2, 512, 128), BF),
            pltpu.VMEM((CHUNKS, 8, 128, 512), F32),
            pltpu.VMEM((CHUNKS, 7, 128, 512), BF),
            pltpu.VMEM((CHUNKS, 7, 128, 512), BF),
            pltpu.VMEM((CHUNKS, 8, 128, 256), BF),
            pltpu.VMEM((2, 2, 4, 512), F32),
            pltpu.VMEM((4, 4, 512), F32),
            dma((6 + CHUNKS,)),
            dma((7,)), dma((7,)),
            dma((CHUNKS, 3)), dma((CHUNKS, 3)),
            dma((CHUNKS, 2)), dma((CHUNKS, 2)),
            dma, dma,
            dma((CHUNKS, 7)), dma((CHUNKS, 7)),
            dma((CHUNKS, 7)), dma((CHUNKS, 7)),
            dma((3,)), dma((3,)),
        ],
        compiler_params=pltpu.CompilerParams(
            collective_id=0, has_side_effects=True, vmem_limit_bytes=60 * 1024 * 1024
        ),
        cost_estimate=pl.CostEstimate(
            flops=6 * 1024 ** 3, bytes_accessed=12 * 1024 ** 2, transcendentals=2 * 1024 * 512
        ),
    )(hidden_in, full_weights.reshape(512, 2048), tiles_of(codes), tiles_of(scales))
    return out[:, None, :]


def solution(mesh):
    return jax.shard_map(
        per_device,
        mesh=mesh,
        in_specs=(P("dp", None), P("mp", "grp", "dp"), P("mp", None, "dp"), P("mp", None, "dp")),
        out_specs=P("mp", "grp", "dp"),
        check_vma=False,
    )
```

```python
import jax
import jax.numpy as jnp
from jax import lax
from jax.experimental import pallas as pl
from jax.experimental.pallas import tpu as pltpu
from jax.sharding import PartitionSpec as P

BF = jnp.bfloat16
F32 = jnp.float32
CHUNKS = 4
PARTS = 1
ROWS = 128 // PARTS
PERIOD = 1.0
SHIFT = 0.0


def multiple(value, of=128):
    return pl.multiple_of(value, of)


def sigmoid(v):
    return 1.0 / (1.0 + jnp.exp(-v))


def kernel(
    hidden, full, codes, scales, out,
    x_all, x_turned, w_teacher, offsets, w_student, code_own, code_next, code_prev,
    scale_all, scale_in, send_offsets, partial, stage, landed, grads, results, gathered,
    local_sem, x_send, x_recv, t_send, t_recv, s_send, s_recv, c_send, c_recv,
    r_send, r_recv, g_send, g_recv, o_send, o_recv,
):
    hi = lax.axis_index("grp")
    dp = lax.axis_index("dp")
    mp = lax.axis_index("mp")
    lo, z = mp // 8, lax.rem(mp, 8)
    y, core = dp // 2, lax.rem(dp, 2)
    x = hi * 2 + lo
    way = 1 - 2 * core

    def at(x=x, y=y, z=z, core=core):
        return (x // 2, y * 2 + core, lax.rem(x, 2) * 8 + z)

    x_next, x_prev, x_far = lax.rem(x + 1, 4), lax.rem(x + 3, 4), lax.rem(x + 2, 4)
    y_fwd, y_bwd, y_far = lax.rem(y + 4 + way, 4), lax.rem(y + 4 - way, 4), lax.rem(y + 2, 4)

    def zed(step):
        return lax.rem(z + 8 + way * step, 8)

    sibling = at(core=1 - core)
    to_y_fwd, to_y_bwd, to_y_far = at(y=y_fwd), at(y=y_bwd), at(y=y_far)
    to_x = [at(x=x_next), at(x=x_prev), at(x=x_far)]
    x_of = [x_next, x_prev, x_far]
    to_z_fwd, to_z_bwd = at(z=zed(1)), at(z=zed(-1))

    sent = []

    def send(src, dst, send_sem, recv_sem, device):
        copy = pltpu.make_async_remote_copy(
            src_ref=src, dst_ref=dst, send_sem=send_sem, recv_sem=recv_sem,
            device_id=device, device_id_type=pl.DeviceIdType.MESH,
        )
        copy.start()
        sent.append(copy)

    def arrived(ref, send_sem, recv_sem):
        pltpu.make_async_remote_copy(
            src_ref=ref, dst_ref=ref, send_sem=send_sem, recv_sem=recv_sem,
            device_id=sibling, device_id_type=pl.DeviceIdType.MESH,
        ).wait_recv()

    def local(src, dst, index):
        copy = pltpu.make_async_copy(src, dst, local_sem.at[index])
        copy.start()
        return copy

    def token_rows(block):
        return x_all.at[pl.ds(multiple(block * 128), 128), :]

    def own_columns(ref, chunk):
        return ref.at[chunk, lo, :, pl.ds(multiple(hi * 128), 128)]

    def teacher_columns(which, chunk):
        return full.at[:, pl.ds(multiple(which * 512 + chunk * 128), 128)]

    hidden_copies = [
        local(
            hidden.at[:, pl.ds(multiple(z * 512 + half * 4096), 512)],
            x_all.at[pl.ds(multiple(dp * 128), 128), pl.ds(half * 512, 512)],
            half,
        )
        for half in range(2)
    ]
    next_copy = local(codes.at[:, x_next], code_next, 2)
    prev_copy = local(codes.at[:, x_prev], code_prev, 3)
    scale_copy = local(scales, scale_in, 4)
    own_copy = local(codes.at[:, x], code_own, 5)
    teacher_copies = [
        local(teacher_columns(x, c), own_columns(w_teacher, c), 6 + c) for c in range(CHUNKS)
    ]

    barrier = pltpu.get_barrier_semaphore()
    for device in [sibling, to_y_fwd, to_y_bwd, to_y_far, to_z_fwd, to_z_bwd] + to_x:
        pl.semaphore_signal(barrier, inc=1, device_id=device, device_id_type=pl.DeviceIdType.MESH)
    pl.semaphore_wait(barrier, 9)

    def send_teacher(c):
        for j in (2, 0, 1):
            send(teacher_columns(x_of[j], c), own_columns(w_teacher, c),
                 t_send.at[c, j], t_recv.at[c, j], to_x[j])

    def code_offsets(ref, c, k):
        rows = ref.reshape(512 * 8, 128)[pl.ds(c * 2 + k, 512, stride=8), :]
        return (rows.astype(F32) - 1.5).astype(BF)

    def send_student(c):
        for j, ref in ((0, code_next), (1, code_prev)):
            low, high = code_offsets(ref, c, 0), code_offsets(ref, c, 1)
            send_offsets[c, j] = jnp.where(hi == 0, low, high)
            send(send_offsets.at[c, j], own_columns(offsets, c),
                 s_send.at[c, j], s_recv.at[c, j], to_x[j])

    def own_offsets(c):
        for k in range(2):
            offsets[c, lo, :, k * 128:(k + 1) * 128] = code_offsets(code_own, c, k)

    send_teacher(0)
    for copy in hidden_copies:
        copy.wait()
    mine = token_rows(dp)
    send(mine, mine, x_send.at[0], x_recv.at[0], to_y_fwd)
    send(mine, mine, x_send.at[1], x_recv.at[1], to_y_bwd)
    send(mine, mine, x_send.at[3], x_recv.at[3], to_y_far)
    send(mine, mine, x_send.at[2], x_recv.at[2], sibling)
    next_copy.wait()
    prev_copy.wait()
    send_student(0)
    scale_copy.wait()
    scale_all[lo] = scale_in[:, x]
    send(scale_in.at[:, x_next], scale_all.at[lo], c_send, c_recv, to_x[0])
    send_teacher(1)
    send_student(1)
    own_copy.wait()
    for c in range(CHUNKS):
        own_offsets(c)

    behind, ahead, far = (token_rows(b * 2 + core) for b in (y_bwd, y_fwd, y_far))
    arrived(behind, x_send.at[0], x_recv.at[0])
    send(behind, behind, x_send.at[4], x_recv.at[4], sibling)
    arrived(ahead, x_send.at[1], x_recv.at[1])
    send(ahead, ahead, x_send.at[5], x_recv.at[5], sibling)
    arrived(far, x_send.at[3], x_recv.at[3])
    send(far, far, x_send.at[6], x_recv.at[6], sibling)
    other = 1 - core
    for b, i in ((y, 2), (y_fwd, 4), (y_bwd, 5), (y_far, 6)):
        arrived(token_rows(b * 2 + other), x_send.at[i], x_recv.at[i])

    def project(c):
        teacher_copies[c].wait()
        for j, origin in ((0, x_prev), (1, x_next), (2, x_far)):
            block = w_teacher.at[
                c, lax.rem(origin, 2), :, pl.ds(multiple((origin // 2) * 128), 128)
            ]
            arrived(block, t_send.at[c, j], t_recv.at[c, j])
        for j, origin in ((0, x_prev), (1, x_next)):
            block = offsets.at[
                c, lax.rem(origin, 2), :, pl.ds(multiple((origin // 2) * 128), 128)
            ]
            arrived(block, s_send.at[c, j], s_recv.at[c, j])
        if c == 0:
            arrived(scale_all.at[1 - lo], c_send, c_recv)
        if c + 2 < CHUNKS:
            send_teacher(c + 2)
            send_student(c + 2)
        for half in range(2):
            for group in range(4):
                line = jnp.concatenate(
                    [scale_all[half, group, c * 2 + k:c * 2 + k + 1, :] for k in range(2)], axis=1
                )
                rows = pl.ds(half * 512 + group * 128, 128)
                values = offsets[c, half, group * 128:(group + 1) * 128, :].astype(F32)
                w_student[rows, :] = (values * line).astype(BF)
        teacher = w_teacher.at[c].reshape(1024, 256)

        @pl.loop(0, 4)
        def _(i):
            tokens = x_all[pl.ds(multiple(i * 256, 256), 256), :]
            student_part = jnp.dot(tokens, w_student[...], preferred_element_type=F32)
            teacher_part = jnp.dot(tokens, teacher[...], preferred_element_type=F32)
            gap = student_part - teacher_part
            for h in range(2):
                part = slice(h * 128, (h + 1) * 128)
                partial[c, i * 2 + h, :, 0:256] = student_part[part]
                partial[c, i * 2 + h, :, 256:512] = gap[part]

    def begin(c, part):
        pass_on(c, part, 0, zed(4), None, to_z_fwd)
        pass_on(c, part, 4, zed(-3), None, to_z_bwd)

    def lines(part):
        return slice(part * ROWS, (part + 1) * ROWS)

    def pass_on(c, part, index, owner, before, device):
        total = partial[c, owner, lines(part), :]
        if before is not None:
            total = total + landed[c, part, before].astype(F32)
        stage[c, part, index] = total.astype(BF)
        send(stage.at[c, part, index], landed.at[c, part, index],
             r_send.at[c, part, index], r_recv.at[c, part, index], device)

    def summed(c, part, index):
        arrived(landed.at[c, part, index], r_send.at[c, part, index], r_recv.at[c, part, index])

    def reduce_step(c, part, step):
        summed(c, part, step - 1)
        if step < 4:
            pass_on(c, part, step, zed(4 - step), step - 1, to_z_fwd)
            summed(c, part, 3 + step)
            if step < 3:
                pass_on(c, part, 4 + step, zed(step - 3), 3 + step, to_z_bwd)
            return
        total = (partial[c, z, lines(part), :] + landed[c, part, 3].astype(F32)
                 + landed[c, part, 6].astype(F32))
        gate, upper = total[:, 0:128], total[:, 128:256]
        teacher_gate, teacher_upper = gate - total[:, 256:384], upper - total[:, 384:512]
        sig = sigmoid(gate)
        student_hidden = gate * sig * upper
        teacher_hidden = teacher_gate * sigmoid(teacher_gate) * teacher_upper
        difference = (student_hidden - teacher_hidden) * (1.0 / 1024.0)
        grads[c, z, lines(part), 0:128] = (difference * upper * sig * (1.0 + gate * (1.0 - sig))).astype(BF)
        grads[c, z, lines(part), 128:256] = (difference * gate * sig).astype(BF)
        share(c, part, z, 0, to_z_fwd)
        share(c, part, z, 4, to_z_bwd)

    def share(c, part, owner, index, device):
        block = grads.at[c, owner, lines(part), :]
        send(block, block, g_send.at[c, part, index], g_recv.at[c, part, index], device)

    def shared(c, part, owner, index):
        arrived(grads.at[c, owner, lines(part), :],
                g_send.at[c, part, index], g_recv.at[c, part, index])

    def gather_step(c, part, step):
        shared(c, part, zed(-step), step - 1)
        if step < 4:
            share(c, part, zed(-step), step, to_z_fwd)
            shared(c, part, zed(step), 3 + step)
            if step < 3:
                share(c, part, zed(step), 4 + step, to_z_bwd)

    def turn():
        for i in range(8):
            rows = slice(i * 128, (i + 1) * 128)
            x_turned[:, rows] = x_all[rows, :].T

    def back(c):
        all_grads = grads.at[c].reshape(1024, 256)
        for half in range(2):
            rows = x_turned[half * 512:(half + 1) * 512, :]
            weight_grads = jnp.dot(rows, all_grads[...], preferred_element_type=F32)
            weighted = weight_grads * offsets[c, half].astype(F32)
            sums = weighted.reshape(4, 128, 256).sum(axis=1)
            for k in range(2):
                results[k, half, :, c * 128:(c + 1) * 128] = sums[:, k * 128:(k + 1) * 128]

    events = []
    for c in range(CHUNKS):
        start = c * PERIOD
        events.append((start, c, project, ()))
        for part in range(PARTS):
            begun = start + part * SHIFT
            events.append((begun, c, begin, (part,)))
            for step in range(1, 5):
                events.append((begun + step, c, reduce_step, (part, step)))
                events.append((begun + 4 + step, c, gather_step, (part, step)))
        events.append((start + (PARTS - 1) * SHIFT + 8.5, c, back, ()))
    turned = 0
    for _, c, action, rest in sorted(events, key=lambda e: e[:2]):
        action(c, *rest)
        turned += action is begin
        if turned == PARTS:
            turn()
            turned += 1

    for j in range(3):
        send(results.at[x_of[j] // 2, lax.rem(x_of[j], 2)], gathered.at[x],
             o_send.at[j], o_recv.at[j], to_x[j])
    gathered[x] = results[hi, lo]
    for j, origin in ((0, x_prev), (1, x_next), (2, x_far)):
        arrived(gathered.at[origin], o_send.at[j], o_recv.at[j])
    for i in range(4):
        out[:, i * 512:(i + 1) * 512] = gathered[i]
    for copy in sent:
        copy.wait_send()


def tiles_of(array):
    rows = array.shape[0]
    return array.reshape(rows, 2, 4, 4, 128).transpose(0, 2, 3, 1, 4).reshape(rows, 4, 8, 128)


def per_device(hidden_in, full_weights, codes, scales):
    dma = pltpu.SemaphoreType.DMA
    out = pl.pallas_call(
        kernel,
        out_shape=jax.ShapeDtypeStruct((4, 2048), F32),
        in_specs=[pl.BlockSpec(memory_space=pl.ANY)] * 4,
        out_specs=pl.BlockSpec(memory_space=pltpu.VMEM),
        scratch_shapes=[
            pltpu.VMEM((1024, 1024), BF),
            pltpu.VMEM((1024, 1024), BF),
            pltpu.VMEM((CHUNKS, 2, 512, 256), BF),
            pltpu.VMEM((CHUNKS, 2, 512, 256), BF),
            pltpu.VMEM((1024, 256), BF),
            pltpu.VMEM((512, 8, 128), jnp.int32),
            pltpu.VMEM((512, 8, 128), jnp.int32),
            pltpu.VMEM((512, 8, 128), jnp.int32),
            pltpu.VMEM((2, 4, 8, 128), F32),
            pltpu.VMEM((4, 4, 8, 128), F32),
            pltpu.VMEM((CHUNKS, 2, 512, 128), BF),
            pltpu.VMEM((CHUNKS, 8, 128, 512), F32),
            pltpu.VMEM((CHUNKS, PARTS, 7, ROWS, 512), BF),
            pltpu.VMEM((CHUNKS, PARTS, 7, ROWS, 512), BF),
            pltpu.VMEM((CHUNKS, 8, 128, 256), BF),
            pltpu.VMEM((2, 2, 4, 512), F32),
            pltpu.VMEM((4, 4, 512), F32),
            dma((6 + CHUNKS,)),
            dma((7,)), dma((7,)),
            dma((CHUNKS, 3)), dma((CHUNKS, 3)),
            dma((CHUNKS, 2)), dma((CHUNKS, 2)),
            dma, dma,
            dma((CHUNKS, PARTS, 7)), dma((CHUNKS, PARTS, 7)),
            dma((CHUNKS, PARTS, 7)), dma((CHUNKS, PARTS, 7)),
            dma((3,)), dma((3,)),
        ],
        compiler_params=pltpu.CompilerParams(
            collective_id=0, has_side_effects=True, vmem_limit_bytes=60 * 1024 * 1024
        ),
        cost_estimate=pl.CostEstimate(
            flops=6 * 1024 ** 3, bytes_accessed=12 * 1024 ** 2, transcendentals=2 * 1024 * 512
        ),
    )(hidden_in, full_weights.reshape(512, 2048), tiles_of(codes), tiles_of(scales))
    return out[:, None, :]


def solution(mesh):
    return jax.shard_map(
        per_device,
        mesh=mesh,
        in_specs=(P("dp", None), P("mp", "grp", "dp"), P("mp", None, "dp"), P("mp", None, "dp")),
        out_specs=P("mp", "grp", "dp"),
        check_vma=False,
    )
```

```python
import jax
import jax.numpy as jnp
from jax import lax
from jax.experimental import pallas as pl
from jax.experimental.pallas import tpu as pltpu
from jax.sharding import PartitionSpec as P

BF = jnp.bfloat16
F32 = jnp.float32
CHUNKS = 4
STARTS = (0, 1, 2, 3)
EARLY = 4
STRIDES = (3,)
LAG = 0.0
NEWEST = 1
HALVES = [(0, 2, 0, 512), (2, 4, 0, 512)]
WHOLE = [(0, 4, 0, 512)]
MESSAGES = (HALVES, WHOLE, WHOLE, WHOLE)
PLACE = (0, 1, 3, 2)


def multiple(value, of=128):
    return pl.multiple_of(value, of)


def sigmoid(v):
    return 1.0 / (1.0 + jnp.exp(-v))


def kernel(
    hidden, full, codes, scales, out,
    x_all, x_turned, w_teacher, offsets, w_student, code_own, code_next, code_prev,
    scale_all, scale_in, send_offsets, partial, stage, landed, grads, results, gathered,
    local_sem, y_send, y_recv, p_send, p_recv, t_send, t_recv, s_send, s_recv, c_send, c_recv,
    r_send, r_recv, g_send, g_recv, o_send, o_recv,
):
    hi = lax.axis_index("grp")
    dp = lax.axis_index("dp")
    mp = lax.axis_index("mp")
    lo, z = mp // 8, lax.rem(mp, 8)
    y, core = dp // 2, lax.rem(dp, 2)
    x = hi * 2 + lo
    way = 1 - 2 * core

    def at(x=x, y=y, z=z, core=core):
        return (x // 2, y * 2 + core, lax.rem(x, 2) * 8 + z)

    x_next, x_prev, x_far = lax.rem(x + 1, 4), lax.rem(x + 3, 4), lax.rem(x + 2, 4)

    def zed(step):
        return lax.rem(z + 8 + way * step, 8)

    def y_at(turn):
        return lax.rem(y + turn, 4)

    sibling = at(core=1 - core)
    to_x = [at(x=x_next), at(x=x_prev), at(x=x_far)]
    x_of = [x_next, x_prev, x_far]
    to_y = {turn: at(y=y_at(turn)) for turn in (1, 3)}
    to_relay = at(y=lax.rem(y + 4 - way, 4))
    to_z_fwd, to_z_bwd = at(z=zed(1)), at(z=zed(-1))
    to_z_fwd2, to_z_bwd2 = at(z=zed(2)), at(z=zed(-2))

    sent = []

    def send(src, dst, send_sem, recv_sem, device):
        copy = pltpu.make_async_remote_copy(
            src_ref=src, dst_ref=dst, send_sem=send_sem, recv_sem=recv_sem,
            device_id=device, device_id_type=pl.DeviceIdType.MESH,
        )
        copy.start()
        sent.append(copy)

    def arrived(ref, send_sem, recv_sem):
        pltpu.make_async_remote_copy(
            src_ref=ref, dst_ref=ref, send_sem=send_sem, recv_sem=recv_sem,
            device_id=sibling, device_id_type=pl.DeviceIdType.MESH,
        ).wait_recv()

    def local(src, dst, index):
        copy = pltpu.make_async_copy(src, dst, local_sem.at[index])
        copy.start()
        return copy

    def token_rows(place, which):
        return x_all.at[pl.ds(multiple(place * 256 + which * 128), 128), :]

    def own_columns(ref, chunk):
        return ref.at[chunk, lo, :, pl.ds(multiple(hi * 128), 128)]

    def teacher_columns(which, chunk):
        return full.at[:, pl.ds(multiple(which * 512 + chunk * 128), 128)]

    hidden_copies = [
        local(
            hidden.at[:, pl.ds(multiple(z * 512 + half * 4096), 512)],
            x_all.at[pl.ds(multiple(core * 128), 128), pl.ds(half * 512, 512)],
            half,
        )
        for half in range(2)
    ]
    next_copy = local(codes.at[:, x_next], code_next, 2)
    prev_copy = local(codes.at[:, x_prev], code_prev, 3)
    scale_copy = local(scales, scale_in, 4)
    own_copy = local(codes.at[:, x], code_own, 5)
    teacher_copies = [
        local(teacher_columns(x, c), own_columns(w_teacher, c), 6 + c) for c in range(CHUNKS)
    ]

    barrier = pltpu.get_barrier_semaphore()
    for device in [sibling, to_z_fwd, to_z_bwd, to_z_fwd2, to_z_bwd2] + to_x + list(to_y.values()):
        pl.semaphore_signal(barrier, inc=1, device_id=device, device_id_type=pl.DeviceIdType.MESH)

    def send_teacher(c):
        for j in (2, 0, 1):
            send(teacher_columns(x_of[j], c), own_columns(w_teacher, c),
                 t_send.at[c, j], t_recv.at[c, j], to_x[j])

    def code_offsets(ref, c, k):
        rows = ref.reshape(512 * 8, 128)[pl.ds(c * 2 + k, 512, stride=8), :]
        return (rows.astype(F32) - 1.5).astype(BF)

    def prepare_student(c):
        for j, ref in ((0, code_next), (1, code_prev)):
            send_offsets[c, j] = code_offsets(ref, c, hi)

    def send_student(c):
        for j in range(2):
            send(send_offsets.at[c, j], own_columns(offsets, c),
                 s_send.at[c, j], s_recv.at[c, j], to_x[j])

    def own_offsets(c):
        for k in range(2):
            offsets[c, lo, :, k * 128:(k + 1) * 128] = code_offsets(code_own, c, k)

    next_copy.wait()
    prev_copy.wait()
    prepare_student(0)
    scale_copy.wait()
    for copy in hidden_copies:
        copy.wait()
    pl.semaphore_wait(barrier, 10)
    send_student(0)
    send(scale_in.at[:, x_next], scale_all.at[lo], c_send, c_recv, to_x[0])
    mine = token_rows(0, core)
    for turn in (3, 1):
        send(mine, token_rows(PLACE[4 - turn], core),
             y_send.at[4 - turn], y_recv.at[4 - turn], to_y[turn])
    send(mine, mine, p_send.at[0], p_recv.at[0], sibling)
    send_teacher(0)
    for c in range(1, EARLY):
        prepare_student(c)
        send_student(c)
        send_teacher(c)
    scale_all[lo] = scale_in[:, x]
    own_copy.wait()
    own_offsets(0)

    def take_tokens(turn):
        rows = token_rows(PLACE[turn], core)
        arrived(rows, y_send.at[turn], y_recv.at[turn])
        send(rows, rows, p_send.at[turn], p_recv.at[turn], sibling)

    def relay_tokens():
        send(token_rows(1 + core, core), token_rows(PLACE[2], core),
             y_send.at[2], y_recv.at[2], to_relay)

    def take_sibling(turn):
        arrived(token_rows(PLACE[turn], 1 - core), p_send.at[turn], p_recv.at[turn])

    def take_teacher(c):
        teacher_copies[c].wait()
        for j, origin in ((0, x_prev), (1, x_next), (2, x_far)):
            block = w_teacher.at[
                c, lax.rem(origin, 2), :, pl.ds(multiple((origin // 2) * 128), 128)
            ]
            arrived(block, t_send.at[c, j], t_recv.at[c, j])

    def take_student(c):
        for j, origin in ((0, x_prev), (1, x_next)):
            block = offsets.at[
                c, lax.rem(origin, 2), :, pl.ds(multiple((origin // 2) * 128), 128)
            ]
            arrived(block, s_send.at[c, j], s_recv.at[c, j])
        for half in range(2):
            for group in range(4):
                line = jnp.concatenate(
                    [scale_all[half, group, c * 2 + k:c * 2 + k + 1, :] for k in range(2)], axis=1
                )
                rows = pl.ds(half * 512 + group * 128, 128)
                values = offsets[c, half, group * 128:(group + 1) * 128, :].astype(F32)
                w_student[rows, :] = (values * line).astype(BF)

    def student_rows(c, place):
        tokens = x_all[pl.ds(multiple(place * 256, 256), 256), :]
        sums = jnp.dot(tokens, w_student[...], preferred_element_type=F32)
        partial[c, place, :, :, 0:256] = sums.reshape(8, 32, 256)

    def teacher_rows(c, place):
        tokens = x_all[pl.ds(multiple(place * 256, 256), 256), :]
        weights = w_teacher.at[c].reshape(1024, 256)
        sums = jnp.dot(tokens, weights[...], preferred_element_type=F32).reshape(8, 32, 256)
        partial[c, place, :, :, 256:512] = partial[c, place, :, :, 0:256] - sums

    def begin(c, part):
        pass_on(c, part, 0, zed(4), None, to_z_fwd)
        pass_on(c, part, 4, zed(-3), None, to_z_bwd)

    def project_first(c):
        arrived(scale_all.at[1 - lo], c_send, c_recv)
        take_student(c)
        take_sibling(0)
        student_rows(c, 0)
        take_tokens(1)
        take_tokens(3)
        relay_tokens()
        take_sibling(1)
        student_rows(c, 1)
        take_teacher(c)
        teacher_rows(c, 0)
        teacher_rows(c, 1)
        begin(c, 0)
        take_sibling(3)
        student_rows(c, 2)
        teacher_rows(c, 2)
        take_tokens(2)
        take_sibling(2)
        student_rows(c, 3)
        teacher_rows(c, 3)
        begin(c, 1)
        own_offsets(1)
        send_later(c)

    def send_later(c):
        if EARLY <= c + 2 < CHUNKS:
            prepare_student(c + 2)
            send_student(c + 2)
            send_teacher(c + 2)

    def project(c):
        if c == 0:
            project_first(c)
            return
        take_student(c)
        take_teacher(c)
        send_later(c)

        @pl.loop(0, 4)
        def _(i):
            student_rows(c, i)
            teacher_rows(c, i)

        for part in range(len(MESSAGES[c])):
            begin(c, part)
        if c + 1 < CHUNKS:
            own_offsets(c + 1)

    def piece(ref, c, part, index):
        start, stop, low, high = MESSAGES[c][part]
        return ref.at[c, index, start:stop, :, low:high]

    def own_sums(c, part, owner):
        start, stop, low, high = MESSAGES[c][part]
        return partial[c, start:stop, owner, :, low:high]

    def pass_on(c, part, index, owner, before, device):
        total = own_sums(c, part, owner)
        if before is not None:
            total = total + piece(landed, c, part, before)[...].astype(F32)
        source = piece(stage, c, part, index)
        source[...] = total.astype(BF)
        send(source, piece(landed, c, part, index),
             r_send.at[c, part, index], r_recv.at[c, part, index], device)

    def summed(c, part, index):
        arrived(piece(landed, c, part, index),
                r_send.at[c, part, index], r_recv.at[c, part, index])

    def reduce_step(c, part, step):
        summed(c, part, step - 1)
        pass_on(c, part, step, zed(4 - step), step - 1, to_z_fwd)
        summed(c, part, 3 + step)
        if step < 3:
            pass_on(c, part, 4 + step, zed(step - 3), 3 + step, to_z_bwd)

    def finish(c):
        for part in range(len(MESSAGES[c])):
            summed(c, part, 3)
        total = partial[c, :, z] + landed[c, 3].astype(F32) + landed[c, 6].astype(F32)
        gate, upper = total[:, :, 0:128], total[:, :, 128:256]
        teacher_gate, teacher_upper = gate - total[:, :, 256:384], upper - total[:, :, 384:512]
        sig = sigmoid(gate)
        student_hidden = gate * sig * upper
        teacher_hidden = teacher_gate * sigmoid(teacher_gate) * teacher_upper
        difference = (student_hidden - teacher_hidden) * (1.0 / 1024.0)
        grads[c, :, z, :, 0:128] = (difference * upper * sig * (1.0 + gate * (1.0 - sig))).astype(BF)
        grads[c, :, z, :, 128:256] = (difference * gate * sig).astype(BF)
        share(c, z, 0, to_z_fwd)
        share(c, z, 4, to_z_bwd)
        if c in STRIDES:
            share(c, z, 1, to_z_fwd2)
            share(c, z, 5, to_z_bwd2)

    def share(c, owner, index, device):
        block = grads.at[c, :, owner]
        send(block, block, g_send.at[c, index], g_recv.at[c, index], device)

    def shared(c, owner, index):
        arrived(grads.at[c, :, owner], g_send.at[c, index], g_recv.at[c, index])

    def stride_step(c, step):
        if step == 1:
            shared(c, zed(-2), 1)
            share(c, zed(-2), 2, to_z_fwd)
            share(c, zed(-2), 3, to_z_fwd2)
            shared(c, zed(2), 5)
            share(c, zed(2), 6, to_z_bwd)
        else:
            for index, distance in ((0, -1), (4, 1), (2, -3), (6, 3), (3, -4)):
                shared(c, zed(distance), index)

    def gather_step(c, step):
        shared(c, zed(-step), step - 1)
        if step < 4:
            share(c, zed(-step), step, to_z_fwd)
            shared(c, zed(step), 3 + step)
            if step < 3:
                share(c, zed(step), 4 + step, to_z_bwd)

    def turn():
        for i in range(8):
            rows = slice(i * 128, (i + 1) * 128)
            x_turned[:, rows] = x_all[rows, :].T

    def back(c):
        all_grads = grads.at[c].reshape(1024, 256)
        for half in range(2):
            rows = x_turned[half * 512:(half + 1) * 512, :]
            weight_grads = jnp.dot(rows, all_grads[...], preferred_element_type=F32)
            weighted = weight_grads * offsets[c, half].astype(F32)
            sums = weighted.reshape(4, 128, 256).sum(axis=1)
            for k in range(2):
                results[k, half, :, c * 128:(c + 1) * 128] = sums[:, k * 128:(k + 1) * 128]

    events = []
    for c in range(CHUNKS):
        start = STARTS[c]
        events.append((start, c, project, ()))
        for step in range(1, 4):
            for part in range(len(MESSAGES[c])):
                events.append((start + step, c, reduce_step, (part, step)))
        events.append((start + 4, c, finish, ()))
        for step in range(1, 5):
            when = start + 4 + step + LAG * (CHUNKS - 1 - c)
            if c not in STRIDES:
                events.append((when, c, gather_step, (step,)))
            elif step < 3:
                events.append((when, c, stride_step, (step,)))
        events.append((when + 0.5, c, back, ()))
    for at_time, c, action, rest in sorted(events, key=lambda e: (e[0], NEWEST * e[1])):
        action(c, *rest)
        if at_time == 0:
            turn()
        while at_time >= 6 and len(sent) > 16:
            sent.pop(0).wait_send()

    for j in range(3):
        send(results.at[x_of[j] // 2, lax.rem(x_of[j], 2)], gathered.at[x],
             o_send.at[j], o_recv.at[j], to_x[j])
    gathered[x] = results[hi, lo]
    for j, origin in ((0, x_prev), (1, x_next), (2, x_far)):
        arrived(gathered.at[origin], o_send.at[j], o_recv.at[j])
    for i in range(4):
        out[:, i * 512:(i + 1) * 512] = gathered[i]
    for copy in sent:
        copy.wait_send()


def tiles_of(array):
    rows = array.shape[0]
    return array.reshape(rows, 2, 4, 4, 128).transpose(0, 2, 3, 1, 4).reshape(rows, 4, 8, 128)


def per_device(hidden_in, full_weights, codes, scales):
    dma = pltpu.SemaphoreType.DMA
    out = pl.pallas_call(
        kernel,
        out_shape=jax.ShapeDtypeStruct((4, 2048), F32),
        in_specs=[pl.BlockSpec(memory_space=pl.ANY)] * 4,
        out_specs=pl.BlockSpec(memory_space=pltpu.VMEM),
        scratch_shapes=[
            pltpu.VMEM((1024, 1024), BF),
            pltpu.VMEM((1024, 1024), BF),
            pltpu.VMEM((CHUNKS, 2, 512, 256), BF),
            pltpu.VMEM((CHUNKS, 2, 512, 256), BF),
            pltpu.VMEM((1024, 256), BF),
            pltpu.VMEM((512, 8, 128), jnp.int32),
            pltpu.VMEM((512, 8, 128), jnp.int32),
            pltpu.VMEM((512, 8, 128), jnp.int32),
            pltpu.VMEM((2, 4, 8, 128), F32),
            pltpu.VMEM((4, 4, 8, 128), F32),
            pltpu.VMEM((CHUNKS, 2, 512, 128), BF),
            pltpu.VMEM((CHUNKS, 4, 8, 32, 512), F32),
            pltpu.VMEM((CHUNKS, 7, 4, 32, 512), BF),
            pltpu.VMEM((CHUNKS, 7, 4, 32, 512), BF),
            pltpu.VMEM((CHUNKS, 4, 8, 32, 256), BF),
            pltpu.VMEM((2, 2, 4, 512), F32),
            pltpu.VMEM((4, 4, 512), F32),
            dma((6 + CHUNKS,)),
            dma((4,)), dma((4,)),
            dma((4,)), dma((4,)),
            dma((CHUNKS, 3)), dma((CHUNKS, 3)),
            dma((CHUNKS, 2)), dma((CHUNKS, 2)),
            dma, dma,
            dma((CHUNKS, 2, 7)), dma((CHUNKS, 2, 7)),
            dma((CHUNKS, 7)), dma((CHUNKS, 7)),
            dma((3,)), dma((3,)),
        ],
        compiler_params=pltpu.CompilerParams(
            collective_id=0, has_side_effects=True, vmem_limit_bytes=60 * 1024 * 1024
        ),
        cost_estimate=pl.CostEstimate(
            flops=6 * 1024 ** 3, bytes_accessed=12 * 1024 ** 2, transcendentals=2 * 1024 * 512
        ),
    )(hidden_in, full_weights.reshape(512, 2048), tiles_of(codes), tiles_of(scales))
    return out[:, None, :]


def solution(mesh):
    return jax.shard_map(
        per_device,
        mesh=mesh,
        in_specs=(P("dp", None), P("mp", "grp", "dp"), P("mp", None, "dp"), P("mp", None, "dp")),
        out_specs=P("mp", "grp", "dp"),
        check_vma=False,
    )
```

```python
import jax
import jax.numpy as jnp
from jax import lax
from jax.experimental import pallas as pl
from jax.experimental.pallas import tpu as pltpu
from jax.sharding import PartitionSpec as P

BF = jnp.bfloat16
F32 = jnp.float32
CHUNKS = 4
STARTS = (0, 1, 2, 3)
EARLY = 4
STRIDES = (3,)
LAG = -0.3
NEWEST = 1
HALVES = [(0, 2, 0, 512), (2, 4, 0, 512)]
WHOLE = [(0, 4, 0, 512)]
MESSAGES = (HALVES, WHOLE, WHOLE, WHOLE)
PLACE = (0, 1, 3, 2)


def multiple(value, of=128):
    return pl.multiple_of(value, of)


def sigmoid(v):
    return 1.0 / (1.0 + jnp.exp(-v))


def kernel(
    hidden, full, codes, scales, out,
    x_all, x_turned, w_teacher, offsets, w_student, code_own, code_next, code_prev,
    scale_all, scale_in, send_offsets, partial, stage, landed, grads, results, gathered,
    local_sem, y_send, y_recv, p_send, p_recv, t_send, t_recv, s_send, s_recv, c_send, c_recv,
    r_send, r_recv, g_send, g_recv, o_send, o_recv,
):
    hi = lax.axis_index("grp")
    dp = lax.axis_index("dp")
    mp = lax.axis_index("mp")
    lo, z = mp // 8, lax.rem(mp, 8)
    y, core = dp // 2, lax.rem(dp, 2)
    x = hi * 2 + lo
    way = 1 - 2 * core

    def at(x=x, y=y, z=z, core=core):
        return (x // 2, y * 2 + core, lax.rem(x, 2) * 8 + z)

    x_next, x_prev, x_far = lax.rem(x + 1, 4), lax.rem(x + 3, 4), lax.rem(x + 2, 4)

    def zed(step):
        return lax.rem(z + 8 + way * step, 8)

    def y_at(turn):
        return lax.rem(y + turn, 4)

    sibling = at(core=1 - core)
    to_x = [at(x=x_next), at(x=x_prev), at(x=x_far)]
    x_of = [x_next, x_prev, x_far]
    to_y = {turn: at(y=y_at(turn)) for turn in (1, 3)}
    to_relay = at(y=lax.rem(y + 4 - way, 4))
    to_z_fwd, to_z_bwd = at(z=zed(1)), at(z=zed(-1))
    to_z_fwd2, to_z_bwd2 = at(z=zed(2)), at(z=zed(-2))

    sent = []

    def send(src, dst, send_sem, recv_sem, device):
        copy = pltpu.make_async_remote_copy(
            src_ref=src, dst_ref=dst, send_sem=send_sem, recv_sem=recv_sem,
            device_id=device, device_id_type=pl.DeviceIdType.MESH,
        )
        copy.start()
        sent.append(copy)

    def arrived(ref, send_sem, recv_sem):
        pltpu.make_async_remote_copy(
            src_ref=ref, dst_ref=ref, send_sem=send_sem, recv_sem=recv_sem,
            device_id=sibling, device_id_type=pl.DeviceIdType.MESH,
        ).wait_recv()

    def local(src, dst, index):
        copy = pltpu.make_async_copy(src, dst, local_sem.at[index])
        copy.start()
        return copy

    def token_rows(place, which):
        return x_all.at[pl.ds(multiple(place * 256 + which * 128), 128), :]

    def own_columns(ref, chunk):
        return ref.at[chunk, lo, :, pl.ds(multiple(hi * 128), 128)]

    def teacher_columns(which, chunk):
        return full.at[:, pl.ds(multiple(which * 512 + chunk * 128), 128)]

    hidden_copies = [
        local(
            hidden.at[:, pl.ds(multiple(z * 512 + half * 4096), 512)],
            x_all.at[pl.ds(multiple(core * 128), 128), pl.ds(half * 512, 512)],
            half,
        )
        for half in range(2)
    ]
    next_copy = local(codes.at[:, x_next], code_next, 2)
    prev_copy = local(codes.at[:, x_prev], code_prev, 3)
    scale_copy = local(scales, scale_in, 4)
    own_copy = local(codes.at[:, x], code_own, 5)
    teacher_copies = [
        local(teacher_columns(x, c), own_columns(w_teacher, c), 6 + c) for c in range(CHUNKS)
    ]

    barrier = pltpu.get_barrier_semaphore()
    for device in [sibling, to_z_fwd, to_z_bwd, to_z_fwd2, to_z_bwd2] + to_x + list(to_y.values()):
        pl.semaphore_signal(barrier, inc=1, device_id=device, device_id_type=pl.DeviceIdType.MESH)

    def send_teacher(c):
        for j in (2, 0, 1):
            send(teacher_columns(x_of[j], c), own_columns(w_teacher, c),
                 t_send.at[c, j], t_recv.at[c, j], to_x[j])

    def code_offsets(ref, c, k):
        rows = ref.reshape(512 * 8, 128)[pl.ds(c * 2 + k, 512, stride=8), :]
        return (rows.astype(F32) - 1.5).astype(BF)

    def prepare_student(c):
        for j, ref in ((0, code_next), (1, code_prev)):
            send_offsets[c, j] = code_offsets(ref, c, hi)

    def send_student(c):
        for j in range(2):
            send(send_offsets.at[c, j], own_columns(offsets, c),
                 s_send.at[c, j], s_recv.at[c, j], to_x[j])

    def own_offsets(c):
        for k in range(2):
            offsets[c, lo, :, k * 128:(k + 1) * 128] = code_offsets(code_own, c, k)

    next_copy.wait()
    prev_copy.wait()
    prepare_student(0)
    scale_copy.wait()
    for copy in hidden_copies:
        copy.wait()
    pl.semaphore_wait(barrier, 10)
    send_student(0)
    send(scale_in.at[:, x_next], scale_all.at[lo], c_send, c_recv, to_x[0])
    mine = token_rows(0, core)
    for turn in (3, 1):
        send(mine, token_rows(PLACE[4 - turn], core),
             y_send.at[4 - turn], y_recv.at[4 - turn], to_y[turn])
    send(mine, mine, p_send.at[0], p_recv.at[0], sibling)
    send_teacher(0)
    for c in range(1, EARLY):
        prepare_student(c)
        send_student(c)
        send_teacher(c)
    scale_all[lo] = scale_in[:, x]
    own_copy.wait()
    own_offsets(0)

    def take_tokens(turn):
        rows = token_rows(PLACE[turn], core)
        arrived(rows, y_send.at[turn], y_recv.at[turn])
        send(rows, rows, p_send.at[turn], p_recv.at[turn], sibling)

    def relay_tokens():
        send(token_rows(1 + core, core), token_rows(PLACE[2], core),
             y_send.at[2], y_recv.at[2], to_relay)

    def take_sibling(turn):
        arrived(token_rows(PLACE[turn], 1 - core), p_send.at[turn], p_recv.at[turn])

    def take_teacher(c):
        teacher_copies[c].wait()
        for j, origin in ((0, x_prev), (1, x_next), (2, x_far)):
            block = w_teacher.at[
                c, lax.rem(origin, 2), :, pl.ds(multiple((origin // 2) * 128), 128)
            ]
            arrived(block, t_send.at[c, j], t_recv.at[c, j])

    def take_student(c):
        for j, origin in ((0, x_prev), (1, x_next)):
            block = offsets.at[
                c, lax.rem(origin, 2), :, pl.ds(multiple((origin // 2) * 128), 128)
            ]
            arrived(block, s_send.at[c, j], s_recv.at[c, j])
        for half in range(2):
            for group in range(4):
                line = jnp.concatenate(
                    [scale_all[half, group, c * 2 + k:c * 2 + k + 1, :] for k in range(2)], axis=1
                )
                rows = pl.ds(half * 512 + group * 128, 128)
                values = offsets[c, half, group * 128:(group + 1) * 128, :].astype(F32)
                w_student[rows, :] = (values * line).astype(BF)

    def student_rows(c, place):
        tokens = x_all[pl.ds(multiple(place * 256, 256), 256), :]
        sums = jnp.dot(tokens, w_student[...], preferred_element_type=F32)
        partial[c, place, :, :, 0:256] = sums.reshape(8, 32, 256)

    def teacher_rows(c, place):
        tokens = x_all[pl.ds(multiple(place * 256, 256), 256), :]
        weights = w_teacher.at[c].reshape(1024, 256)
        sums = jnp.dot(tokens, weights[...], preferred_element_type=F32).reshape(8, 32, 256)
        partial[c, place, :, :, 256:512] = partial[c, place, :, :, 0:256] - sums

    def begin(c, part):
        pass_on(c, part, 0, zed(4), None, to_z_fwd)
        pass_on(c, part, 4, zed(-3), None, to_z_bwd)

    def project_first(c):
        arrived(scale_all.at[1 - lo], c_send, c_recv)
        take_student(c)
        take_sibling(0)
        student_rows(c, 0)
        take_tokens(1)
        take_tokens(3)
        relay_tokens()
        take_sibling(1)
        student_rows(c, 1)
        take_teacher(c)
        teacher_rows(c, 0)
        teacher_rows(c, 1)
        begin(c, 0)
        take_sibling(3)
        student_rows(c, 2)
        teacher_rows(c, 2)
        take_tokens(2)
        take_sibling(2)
        student_rows(c, 3)
        teacher_rows(c, 3)
        begin(c, 1)
        own_offsets(1)
        send_later(c)

    def send_later(c):
        if EARLY <= c + 2 < CHUNKS:
            prepare_student(c + 2)
            send_student(c + 2)
            send_teacher(c + 2)

    def project(c):
        if c == 0:
            project_first(c)
            return
        take_student(c)
        take_teacher(c)
        send_later(c)

        @pl.loop(0, 4)
        def _(i):
            student_rows(c, i)
            teacher_rows(c, i)

        for part in range(len(MESSAGES[c])):
            begin(c, part)
        if c + 1 < CHUNKS:
            own_offsets(c + 1)

    def piece(ref, c, part, index):
        start, stop, low, high = MESSAGES[c][part]
        return ref.at[c, index, start:stop, :, low:high]

    def own_sums(c, part, owner):
        start, stop, low, high = MESSAGES[c][part]
        return partial[c, start:stop, owner, :, low:high]

    def pass_on(c, part, index, owner, before, device):
        total = own_sums(c, part, owner)
        if before is not None:
            total = total + piece(landed, c, part, before)[...].astype(F32)
        source = piece(stage, c, part, index)
        source[...] = total.astype(BF)
        send(source, piece(landed, c, part, index),
             r_send.at[c, part, index], r_recv.at[c, part, index], device)

    def summed(c, part, index):
        arrived(piece(landed, c, part, index),
                r_send.at[c, part, index], r_recv.at[c, part, index])

    def reduce_step(c, part, step):
        summed(c, part, step - 1)
        pass_on(c, part, step, zed(4 - step), step - 1, to_z_fwd)
        summed(c, part, 3 + step)
        if step < 3:
            pass_on(c, part, 4 + step, zed(step - 3), 3 + step, to_z_bwd)

    def finish(c):
        for part in range(len(MESSAGES[c])):
            summed(c, part, 3)
        total = partial[c, :, z] + landed[c, 3].astype(F32) + landed[c, 6].astype(F32)
        gate, upper = total[:, :, 0:128], total[:, :, 128:256]
        teacher_gate, teacher_upper = gate - total[:, :, 256:384], upper - total[:, :, 384:512]
        sig = sigmoid(gate)
        student_hidden = gate * sig * upper
        teacher_hidden = teacher_gate * sigmoid(teacher_gate) * teacher_upper
        difference = (student_hidden - teacher_hidden) * (1.0 / 1024.0)
        grads[c, :, z, :, 0:128] = (difference * upper * sig * (1.0 + gate * (1.0 - sig))).astype(BF)
        grads[c, :, z, :, 128:256] = (difference * gate * sig).astype(BF)
        share(c, z, 0, to_z_fwd)
        share(c, z, 4, to_z_bwd)
        if c in STRIDES:
            share(c, z, 1, to_z_fwd2)
            share(c, z, 5, to_z_bwd2)

    def share(c, owner, index, device):
        block = grads.at[c, :, owner]
        send(block, block, g_send.at[c, index], g_recv.at[c, index], device)

    def shared(c, owner, index):
        arrived(grads.at[c, :, owner], g_send.at[c, index], g_recv.at[c, index])

    def stride_step(c, step):
        if step == 1:
            shared(c, zed(-2), 1)
            share(c, zed(-2), 2, to_z_fwd)
            share(c, zed(-2), 3, to_z_fwd2)
            shared(c, zed(2), 5)
            share(c, zed(2), 6, to_z_bwd)
        else:
            for index, distance in ((0, -1), (4, 1), (2, -3), (6, 3), (3, -4)):
                shared(c, zed(distance), index)

    def gather_step(c, step):
        shared(c, zed(-step), step - 1)
        if step < 4:
            share(c, zed(-step), step, to_z_fwd)
            shared(c, zed(step), 3 + step)
            if step < 3:
                share(c, zed(step), 4 + step, to_z_bwd)

    def turn():
        for i in range(8):
            rows = slice(i * 128, (i + 1) * 128)
            x_turned[:, rows] = x_all[rows, :].T

    def back(c):
        all_grads = grads.at[c].reshape(1024, 256)
        for half in range(2):
            rows = x_turned[half * 512:(half + 1) * 512, :]
            weight_grads = jnp.dot(rows, all_grads[...], preferred_element_type=F32)
            weighted = weight_grads * offsets[c, half].astype(F32)
            sums = weighted.reshape(4, 128, 256).sum(axis=1)
            for k in range(2):
                results[k, half, :, c * 128:(c + 1) * 128] = sums[:, k * 128:(k + 1) * 128]

    events = []
    for c in range(CHUNKS):
        start = STARTS[c]
        events.append((start, c, project, ()))
        for step in range(1, 4):
            for part in range(len(MESSAGES[c])):
                events.append((start + step, c, reduce_step, (part, step)))
        events.append((start + 4, c, finish, ()))
        for step in range(1, 5):
            when = start + 4 + step + LAG * (CHUNKS - 1 - c)
            if c not in STRIDES:
                events.append((when, c, gather_step, (step,)))
            elif step < 3:
                events.append((when, c, stride_step, (step,)))
        events.append((when + 0.5, c, back, ()))
    for at_time, c, action, rest in sorted(events, key=lambda e: (e[0], NEWEST * e[1])):
        action(c, *rest)
        if at_time == 0:
            turn()
        while at_time >= 6 and len(sent) > 16:
            sent.pop(0).wait_send()

    for j in range(3):
        send(results.at[x_of[j] // 2, lax.rem(x_of[j], 2)], gathered.at[x],
             o_send.at[j], o_recv.at[j], to_x[j])
    gathered[x] = results[hi, lo]
    for j, origin in ((0, x_prev), (1, x_next), (2, x_far)):
        arrived(gathered.at[origin], o_send.at[j], o_recv.at[j])
    for i in range(4):
        out[:, i * 512:(i + 1) * 512] = gathered[i]
    for copy in sent:
        copy.wait_send()


def tiles_of(array):
    rows = array.shape[0]
    return array.reshape(rows, 2, 4, 4, 128).transpose(0, 2, 3, 1, 4).reshape(rows, 4, 8, 128)


def per_device(hidden_in, full_weights, codes, scales):
    dma = pltpu.SemaphoreType.DMA
    out = pl.pallas_call(
        kernel,
        out_shape=jax.ShapeDtypeStruct((4, 2048), F32),
        in_specs=[pl.BlockSpec(memory_space=pl.ANY)] * 4,
        out_specs=pl.BlockSpec(memory_space=pltpu.VMEM),
        scratch_shapes=[
            pltpu.VMEM((1024, 1024), BF),
            pltpu.VMEM((1024, 1024), BF),
            pltpu.VMEM((CHUNKS, 2, 512, 256), BF),
            pltpu.VMEM((CHUNKS, 2, 512, 256), BF),
            pltpu.VMEM((1024, 256), BF),
            pltpu.VMEM((512, 8, 128), jnp.int32),
            pltpu.VMEM((512, 8, 128), jnp.int32),
            pltpu.VMEM((512, 8, 128), jnp.int32),
            pltpu.VMEM((2, 4, 8, 128), F32),
            pltpu.VMEM((4, 4, 8, 128), F32),
            pltpu.VMEM((CHUNKS, 2, 512, 128), BF),
            pltpu.VMEM((CHUNKS, 4, 8, 32, 512), F32),
            pltpu.VMEM((CHUNKS, 7, 4, 32, 512), BF),
            pltpu.VMEM((CHUNKS, 7, 4, 32, 512), BF),
            pltpu.VMEM((CHUNKS, 4, 8, 32, 256), BF),
            pltpu.VMEM((2, 2, 4, 512), F32),
            pltpu.VMEM((4, 4, 512), F32),
            dma((6 + CHUNKS,)),
            dma((4,)), dma((4,)),
            dma((4,)), dma((4,)),
            dma((CHUNKS, 3)), dma((CHUNKS, 3)),
            dma((CHUNKS, 2)), dma((CHUNKS, 2)),
            dma, dma,
            dma((CHUNKS, 2, 7)), dma((CHUNKS, 2, 7)),
            dma((CHUNKS, 7)), dma((CHUNKS, 7)),
            dma((3,)), dma((3,)),
        ],
        compiler_params=pltpu.CompilerParams(
            collective_id=0, has_side_effects=True, vmem_limit_bytes=60 * 1024 * 1024
        ),
        cost_estimate=pl.CostEstimate(
            flops=6 * 1024 ** 3, bytes_accessed=12 * 1024 ** 2, transcendentals=2 * 1024 * 512
        ),
    )(hidden_in, full_weights.reshape(512, 2048), tiles_of(codes), tiles_of(scales))
    return out[:, None, :]


def solution(mesh):
    return jax.shard_map(
        per_device,
        mesh=mesh,
        in_specs=(P("dp", None), P("mp", "grp", "dp"), P("mp", None, "dp"), P("mp", None, "dp")),
        out_specs=P("mp", "grp", "dp"),
        check_vma=False,
    )
```
